512 devices in a mesh: dp: 32 (over y_lo, z), mp: 16 (over x, y_hi, core).
Axes of the slice: x: 4, y: 4 (y_hi: 2, y_lo: 2; y = y_hi * 2 + y_lo), z: 16, core: 2. Of those that a mesh axis runs over, the one named last changes fastest.
Arguments:
- activations: bfloat16 [49152, 18432], P('dp', 'mp'), may hold values from -6 to 6
- cotangent: bfloat16 [49152, 3072], P('dp', 'mp'), may hold values from -0.03125 to 0.03125
- resident_key_value_weight: bfloat16 [18432, 3072], P('dp', 'mp'), may hold values from -0.75 to 0.75
- down_master: float32 [16, 1152, 128], P('mp', 'dp'), may hold values from -0.75 to 0.75
- down_first: float32 [16, 1152, 128], P('mp', 'dp'), may hold values from -6 to 6
- down_second: float32 [16, 1152, 128], P('mp', 'dp'), may hold values from 1 to 50
- up_master: float32 [16, 192, 128], P('mp', 'dp'), may hold values from -0.75 to 0.75
- up_first: float32 [16, 192, 128], P('mp', 'dp'), may hold values from -6 to 6
- up_second: float32 [16, 192, 128], P('mp', 'dp'), may hold values from 1 to 50
Outputs:
- merged_key_value_weight: bfloat16 [18432, 3072], P('dp', 'mp')
- down_master_new: float32 [16, 1152, 128], P('mp', 'dp')
- down_first_new: float32 [16, 1152, 128], P('mp', 'dp')
- down_second_new: float32 [16, 1152, 128], P('mp', 'dp')
- up_master_new: float32 [16, 192, 128], P('mp', 'dp')
- up_first_new: float32 [16, 192, 128], P('mp', 'dp')
- up_second_new: float32 [16, 192, 128], P('mp', 'dp')
The draws below stay inside these ranges and needn't reach their ends.
All inputs are finite; a program needn't handle non-finite values.
Results may differ from the reference program's by a relative error of at most 0.013.
Values may be sent and summed in bfloat16 or wider, within the bound.
No kernel may reach another device: no remote copies, remote signals or barrier semaphores. Data moves between devices by JAX's collectives and lax.ppermute only.
A program may use at most 64 MiB of HBM per device.

```python
import math
import jax
import jax.numpy as jnp
from jax import lax

D = 18432
KV = 3072
R = 128
TOKENS = 49152
N_MP = 16


def levels(rng, shape, pieces, low, high):
    loudness, own = 1.0, jax.random.fold_in(rng, 6)
    for axis_at, shards_of in pieces:
        draws = jnp.exp(jax.random.uniform(jax.random.fold_in(own, axis_at), (shards_of,), jnp.float32, low / len(pieces), high / len(pieces)))
        loudness = loudness * jnp.repeat(draws, shape[axis_at] // shards_of).reshape([-1 if axis == axis_at else 1 for axis in range(len(shape))])
    return loudness


def normal_values(own_key, shape, width, most, cuts=(), dtype=jnp.bfloat16):
    factor_of = levels(own_key, shape, cuts, -0.22, 0.18) if cuts else 1.0
    result = jax.random.normal(own_key, shape, jnp.float32) * width * factor_of
    return jnp.minimum(jnp.maximum(result, -most), most).astype(dtype)


def setup_inputs(seed: int = 0) -> dict:
    keys = jax.random.split(jax.random.key(seed), 10)
    activations = normal_values(keys[0], (TOKENS, D), 1.0, 6.0, ((0, 32), (1, 16)))
    cotangent = normal_values(keys[1], (TOKENS, KV), (0.5 * TOKENS ** -0.5), 0.03125, ((0, 32), (1, 16)))
    resident_key_value_weight = normal_values(keys[2], (D, KV), 0.05, 0.75, ((0, 32), (1, 16)))
    down_master = normal_values(keys[3], (N_MP, D // N_MP, R), 0.05, 0.75, ((0, 16), (1, 32)), jnp.float32)
    down_first = normal_values(keys[4], (N_MP, D // N_MP, R), 2.0, 6.0, ((0, 16), (1, 32)), jnp.float32)
    down_second = jnp.clip(jnp.exp(math.log(50.0) - 3.912023 * jax.random.uniform(keys[5], (N_MP, D // N_MP, R), jnp.float32) ** levels(keys[5], (N_MP, D // N_MP, R), ((0, 16), (1, 32)), -0.2, 0.2)), 1.0, 50.0)
    up_master = normal_values(keys[6], (N_MP, KV // N_MP, R), 0.05, 0.75, ((0, 16), (1, 32)), jnp.float32)
    up_first = normal_values(keys[7], (N_MP, KV // N_MP, R), 2.0, 6.0, ((0, 16), (1, 32)), jnp.float32)
    up_second = jnp.clip(jnp.exp(math.log(50.0) - 3.912023 * jax.random.uniform(keys[8], (N_MP, KV // N_MP, R), jnp.float32) ** levels(keys[8], (N_MP, KV // N_MP, R), ((0, 16), (1, 32)), -0.2, 0.2)), 1.0, 50.0)
    return {"activations": activations, "cotangent": cotangent, "resident_key_value_weight": resident_key_value_weight, "down_master": down_master, "down_first": down_first, "down_second": down_second, "up_master": up_master, "up_first": up_first, "up_second": up_second}


adapter_scale_factor = 2.0
learn_rate = 0.05
beta_one = 0.9
beta_two = 0.999
adam_eps = 1e-08
decay_rate = 0.01
step_count = 10.0

def adamw_update(master, first, second, grad):
    first_new = beta_one * first + (1.0 - beta_one) * grad
    second_new = beta_two * second + (1.0 - beta_two) * grad * grad
    first_hat = first_new / (1.0 - beta_one ** step_count)
    second_hat = second_new / (1.0 - beta_two ** step_count)
    master_new = master - learn_rate * (first_hat / (jnp.sqrt(second_hat) + adam_eps) + decay_rate * master)
    return (master_new, first_new, second_new)

def reference(activations, cotangent, resident_key_value_weight, down_master, down_first, down_second, up_master, up_first, up_second):
    a_use = down_master.reshape(D, R).astype(jnp.bfloat16)
    bt_use = up_master.reshape(KV, R).astype(jnp.bfloat16)
    hidden = jnp.dot(activations, a_use, preferred_element_type=jnp.float32)
    back = jnp.dot(cotangent, bt_use, preferred_element_type=jnp.float32)
    hidden_activation16 = hidden.astype(jnp.bfloat16)
    backward_half_precision16 = back.astype(jnp.bfloat16)
    down_gradient_matrix = adapter_scale_factor * lax.dot_general(activations, backward_half_precision16, (((0,), (0,)), ((), ())), preferred_element_type=jnp.float32)
    up_gradient_matrix = adapter_scale_factor * lax.dot_general(cotangent, hidden_activation16, (((0,), (0,)), ((), ())), preferred_element_type=jnp.float32)
    down_new = adamw_update(down_master, down_first, down_second, down_gradient_matrix.reshape(down_master.shape))
    up_new = adamw_update(up_master, up_first, up_second, up_gradient_matrix.reshape(up_master.shape))
    a_send = down_new[0].reshape(D, R).astype(jnp.bfloat16)
    bt_send = up_new[0].reshape(KV, R).astype(jnp.bfloat16)
    adapter_difference = lax.dot_general(a_send, bt_send, (((1,), (1,)), ((), ())), preferred_element_type=jnp.float32)
    merged_key_value_weight = (resident_key_value_weight.astype(jnp.float32) + adapter_scale_factor * adapter_difference).astype(jnp.bfloat16)
    return (merged_key_value_weight, down_new[0], down_new[1], down_new[2], up_new[0], up_new[1], up_new[2])
```

```python
import jax
import jax.numpy as jnp
from jax import lax
from jax.experimental import pallas as pl
from jax.experimental.pallas import tpu as pltpu
from jax.sharding import Mesh
from jax.sharding import PartitionSpec as P

adapter_scale_factor = 2.0
learn_rate = 0.05
beta_one = 0.9
beta_two = 0.999
adam_eps = 1e-08
decay_rate = 0.01
step_count = 10.0

BF = jnp.bfloat16
F32 = jnp.float32
DOWN, UP, UP_AT, SLOT = 36, 6, 40, 48
N_YL, N_Z, N_MP = 2, 16, 16
N_DP = N_YL * N_Z
RANK = 128

VMEM = pl.BlockSpec(memory_space=pltpu.VMEM)
SMEM = pl.BlockSpec(memory_space=pltpu.SMEM)


def adamw_update(master, first, second, grad):
    first_new = beta_one * first + (1.0 - beta_one) * grad
    second_new = beta_two * second + (1.0 - beta_two) * grad * grad
    first_hat = first_new / (1.0 - beta_one**step_count)
    second_hat = second_new / (1.0 - beta_two**step_count)
    master_new = master - learn_rate * (
        first_hat / (jnp.sqrt(second_hat) + adam_eps) + decay_rate * master
    )
    return (master_new, first_new, second_new)


def kernel_call(body, out_shape, n_in, scratch=(), smem=(), limit=32 * 2**20):
    many = isinstance(out_shape, (list, tuple))
    return pl.pallas_call(
        body,
        out_shape=out_shape,
        in_specs=[SMEM if i in smem else VMEM for i in range(n_in)],
        out_specs=[VMEM] * len(out_shape) if many else VMEM,
        scratch_shapes=list(scratch),
        compiler_params=pltpu.CompilerParams(vmem_limit_bytes=limit),
    )


def spread_factors(down_ref, up_ref, out_ref, slot):
    slot[...] = jnp.zeros_like(slot)
    slot[0:DOWN, :] = down_ref[0]
    slot[UP_AT : UP_AT + UP, :] = up_ref[0]
    value = slot[...].astype(BF)
    for j in range(out_ref.shape[0]):
        out_ref[j] = value


def project(slots_ref, act_ref, cot_ref, out_ref, down, up):
    for j in range(N_DP):
        value = slots_ref[j].astype(F32)
        down[j * DOWN : j * DOWN + DOWN, :] = value[0:DOWN]
        up[j * UP : j * UP + UP, :] = value[UP_AT : UP_AT + UP]
    a_use = down[...].astype(BF)
    bt_use = up[...].astype(BF)
    rows = out_ref.shape[1]
    step = 4
    for i in range(0, N_MP, step):
        at = pl.ds(i * rows, step * rows)
        hidden = jnp.dot(act_ref[at, :], a_use, preferred_element_type=F32)
        back = jnp.dot(cot_ref[at, :], bt_use, preferred_element_type=F32)
        out_ref[i : i + step, :, 0:RANK] = hidden.astype(BF).reshape(step, rows, RANK)
        out_ref[i : i + step, :, RANK:] = back.astype(BF).reshape(step, rows, RANK)


def add_parts(parts_ref, out_ref):
    total = parts_ref[0].astype(F32)
    for j in range(1, parts_ref.shape[0]):
        total += parts_ref[j].astype(F32)
    value = total.astype(BF)
    for j in range(out_ref.shape[0]):
        out_ref[j] = value


def gradients(full_ref, act_ref, cot_ref, out_ref, down, up, slot):
    tokens = act_ref.shape[0]
    full = full_ref[...].reshape(tokens, 2 * RANK)
    over_tokens = (((0,), (0,)), ((), ()))
    hidden, back = full[:, 0:RANK], full[:, RANK:]
    down[...] = adapter_scale_factor * lax.dot_general(
        act_ref[...], back, over_tokens, preferred_element_type=F32
    )
    up[...] = adapter_scale_factor * lax.dot_general(
        cot_ref[...], hidden, over_tokens, preferred_element_type=F32
    )
    slot[...] = jnp.zeros_like(slot)
    for j in range(N_DP):
        slot[0:DOWN, :] = down[j * DOWN : j * DOWN + DOWN, :]
        slot[UP_AT : UP_AT + UP, :] = up[j * UP : j * UP + UP, :]
        out_ref[j] = slot[...].astype(BF)


def update(
    parts_ref, dm_ref, df_ref, ds_ref, um_ref, uf_ref, us_ref,
    dm_out, df_out, ds_out, um_out, uf_out, us_out, send_out, slot,
):
    total = parts_ref[0].astype(F32)
    for j in range(1, parts_ref.shape[0]):
        total += parts_ref[j].astype(F32)
    down_new = adamw_update(dm_ref[0], df_ref[0], ds_ref[0], total[0:DOWN])
    up_new = adamw_update(um_ref[0], uf_ref[0], us_ref[0], total[UP_AT : UP_AT + UP])
    dm_out[0], df_out[0], ds_out[0] = down_new
    um_out[0], uf_out[0], us_out[0] = up_new
    slot[...] = jnp.zeros_like(slot)
    slot[0:DOWN, :] = down_new[0]
    slot[UP_AT : UP_AT + UP, :] = up_new[0]
    value = slot[...].astype(BF)
    for j in range(send_out.shape[0]):
        send_out[j] = value


def route(place_ref, plane_ref, out_ref, slot):
    y_lo, mp = place_ref[0], place_ref[1]
    low = plane_ref[mp].astype(F32)
    high = plane_ref[N_MP + mp].astype(F32)
    slot[DOWN : DOWN + UP, :] = low[UP_AT : UP_AT + UP]
    slot[DOWN + UP : DOWN + 2 * UP, :] = high[UP_AT : UP_AT + UP]
    for z_to in range(N_Z):
        owner = (z_to % 2) * N_MP + y_lo * (N_MP // 2) + z_to // 2
        slot[0:DOWN, :] = plane_ref[owner].astype(F32)[0:DOWN]
        out_ref[z_to] = slot[...].astype(BF)


def merge(slots_ref, base_ref, out_ref, down, up):
    half = N_Z * UP
    for z in range(N_Z):
        value = slots_ref[z].astype(F32)
        down[z * DOWN : z * DOWN + DOWN, :] = value[0:DOWN]
        up[z * UP : z * UP + UP, :] = value[DOWN : DOWN + UP]
        up[half + z * UP : half + z * UP + UP, :] = value[DOWN + UP : DOWN + 2 * UP]
    difference = lax.dot_general(
        down[...].astype(BF),
        up[...].astype(BF),
        (((1,), (1,)), ((), ())),
        preferred_element_type=F32,
    )
    out_ref[...] = (base_ref[...].astype(F32) + adapter_scale_factor * difference).astype(BF)


def shards(
    activations,
    cotangent,
    resident_key_value_weight,
    down_master,
    down_first,
    down_second,
    up_master,
    up_first,
    up_second,
):
    tokens, features = activations.shape
    heads = cotangent.shape[1]
    shape = jax.ShapeDtypeStruct

    def exchange(value, axes):
        return lax.all_to_all(value, axes, 0, 0, tiled=True)

    own = kernel_call(
        spread_factors, shape((N_DP, SLOT, RANK), BF), 2, [pltpu.VMEM((SLOT, RANK), F32)]
    )(down_master, up_master)
    factors = exchange(own, ("yl", "z"))
    parts = kernel_call(
        project,
        shape((N_MP, tokens // N_MP, 2 * RANK), BF),
        3,
        [pltpu.VMEM((features, RANK), F32), pltpu.VMEM((heads, RANK), F32)],
    )(factors, activations, cotangent)
    parts = exchange(parts, "mp")
    total = kernel_call(add_parts, shape(parts.shape, BF), 1)(parts)
    full = exchange(total, "mp")
    grads = kernel_call(
        gradients,
        shape((N_DP, SLOT, RANK), BF),
        3,
        [
            pltpu.VMEM((features, RANK), F32),
            pltpu.VMEM((heads, RANK), F32),
            pltpu.VMEM((SLOT, RANK), F32),
        ],
    )(full, activations, cotangent)
    grads = exchange(grads, ("yl", "z"))
    state = (down_master, down_first, down_second, up_master, up_first, up_second)
    *new_state, send = kernel_call(
        update,
        [shape(a.shape, F32) for a in state] + [shape((N_YL * N_MP, SLOT, RANK), BF)],
        7,
        [pltpu.VMEM((SLOT, RANK), F32)],
    )(grads, *state)
    plane = exchange(send, ("yl", "mp"))
    place = jnp.stack([lax.axis_index("yl"), lax.axis_index("mp")]).astype(jnp.int32)
    routed = kernel_call(
        route, shape((N_Z, SLOT, RANK), BF), 2, [pltpu.VMEM((SLOT, RANK), F32)], smem=(0,)
    )(place, plane)
    arrived = exchange(routed, "z")
    merged = kernel_call(
        merge,
        shape(resident_key_value_weight.shape, BF),
        2,
        [pltpu.VMEM((N_Z * DOWN, RANK), F32), pltpu.VMEM((heads, RANK), F32)],
    )(arrived, resident_key_value_weight)
    return (merged, *new_state)


def solution(mesh):
    fine = Mesh(mesh.devices.reshape(N_YL, N_Z, N_MP), ("yl", "z", "mp"))
    dp = ("yl", "z")
    wide, state = P(dp, "mp"), P("mp", dp, None)
    return jax.shard_map(
        shards,
        mesh=fine,
        in_specs=(wide,) * 3 + (state,) * 6,
        out_specs=(wide,) + (state,) * 6,
        check_vma=False,
    )
```

```python
import jax
import jax.numpy as jnp
from jax import lax
from jax.experimental import pallas as pl
from jax.experimental.pallas import tpu as pltpu
from jax.sharding import Mesh
from jax.sharding import PartitionSpec as P

adapter_scale_factor = 2.0
learn_rate = 0.05
beta_one = 0.9
beta_two = 0.999
adam_eps = 1e-08
decay_rate = 0.01
step_count = 10.0

BF = jnp.bfloat16
F32 = jnp.float32
DOWN, UP, UP_AT, SLOT = 36, 6, 40, 48
N_YL, N_Z, N_MP = 2, 16, 16
N_DP = N_YL * N_Z
N_CORE = 2
N_ZQ, N_ZP = 8, 2
RANK = 128

VMEM = pl.BlockSpec(memory_space=pltpu.VMEM)
HBM = pl.BlockSpec(memory_space=pltpu.HBM)
SMEM = pl.BlockSpec(memory_space=pltpu.SMEM)


def adamw_update(master, first, second, grad):
    first_new = beta_one * first + (1.0 - beta_one) * grad
    second_new = beta_two * second + (1.0 - beta_two) * grad * grad
    first_hat = first_new / (1.0 - beta_one**step_count)
    second_hat = second_new / (1.0 - beta_two**step_count)
    master_new = master - learn_rate * (
        first_hat / (jnp.sqrt(second_hat) + adam_eps) + decay_rate * master
    )
    return (master_new, first_new, second_new)


def kernel_call(body, out_shape, n_in, scratch=(), smem=(), hbm=(), limit=32 * 2**20):
    many = isinstance(out_shape, (list, tuple))
    return pl.pallas_call(
        body,
        out_shape=out_shape,
        in_specs=[SMEM if i in smem else HBM if i in hbm else VMEM for i in range(n_in)],
        out_specs=[VMEM] * len(out_shape) if many else VMEM,
        scratch_shapes=list(scratch),
        compiler_params=pltpu.CompilerParams(vmem_limit_bytes=limit),
    )


def spread_factors(down_ref, up_ref, out_ref, slot):
    slot[...] = jnp.zeros_like(slot)
    slot[0:DOWN, :] = down_ref[:, 0, :]
    slot[UP_AT : UP_AT + UP, :] = up_ref[:, 0, :]
    value = slot[...].astype(BF)
    for j in range(out_ref.shape[0]):
        out_ref[j] = value


def unpack(slots_ref, factor, rows, at=0):
    for j in range(slots_ref.shape[0]):
        factor[j * rows : j * rows + rows, :] = slots_ref[j].astype(F32)[at : at + rows]


def fetch(act_in, cot_in, act_ref, cot_ref):
    act_ref[...] = act_in[...]
    cot_ref[...] = cot_in[...]


def project_half(half, a_use, bt_use, act_ref, cot_ref, out_ref):
    groups, rows, _ = out_ref.shape
    tokens = groups * rows
    first = pl.multiple_of(half * tokens, tokens)
    back = lax.dot_general(
        cot_ref[:, pl.ds(first, tokens)],
        bt_use,
        (((0,), (0,)), ((), ())),
        preferred_element_type=F32,
    )
    out_ref[:, :, RANK:] = back.astype(BF).reshape(groups, rows, RANK)
    step = groups // 2
    for i in range(0, groups, step):
        at = pl.ds(pl.multiple_of(first + i * rows, step * rows), step * rows)
        hidden = jnp.dot(act_ref[at, :], a_use, preferred_element_type=F32)
        out_ref[i : i + step, :, 0:RANK] = hidden.astype(BF).reshape(step, rows, RANK)


def project_other(place_ref, slots_ref, act_ref, cot_ref, out_ref, a_ref, bt_ref, down, up):
    unpack(slots_ref, down, DOWN)
    unpack(slots_ref, up, UP, UP_AT)
    a_ref[...] = down[...].astype(BF)
    bt_ref[...] = up[...].astype(BF)
    project_half(1 - place_ref[0], a_ref[...], bt_ref[...], act_ref, cot_ref, out_ref)


def project_own(place_ref, a_ref, bt_ref, act_ref, cot_ref, out_ref):
    project_half(place_ref[0], a_ref[...], bt_ref[...], act_ref, cot_ref, out_ref)


def sum_parts(parts_ref):
    total = parts_ref[0].astype(F32)
    for j in range(1, parts_ref.shape[0]):
        total += parts_ref[j].astype(F32)
    return total


def add_parts(parts_ref, out_ref):
    value = sum_parts(parts_ref).astype(BF)
    for j in range(out_ref.shape[0]):
        out_ref[j] = value


def add_pair(one_ref, two_ref, out_ref):
    out_ref[...] = (one_ref[...].astype(F32) + two_ref[...].astype(F32)).astype(BF)


def gradients(full_ref, act_ref, cot_ref, out_ref, down, up, slot):
    tokens = act_ref.shape[0]
    full = full_ref[...].reshape(tokens, 2 * RANK)
    hidden, back = full[:, 0:RANK], full[:, RANK:]
    down[...] = adapter_scale_factor * lax.dot_general(
        act_ref[...], back, (((0,), (0,)), ((), ())), preferred_element_type=F32
    )
    up[...] = adapter_scale_factor * jnp.dot(
        cot_ref[...], hidden, preferred_element_type=F32
    )
    for near in range(N_YL * N_ZP):
        y_lo, zp = divmod(near, N_ZP)
        for zq in range(N_ZQ):
            j = y_lo * N_Z + zq * N_ZP + zp
            at = zq * (DOWN + UP)
            slot[at : at + DOWN, :] = down[j * DOWN : j * DOWN + DOWN, :]
            slot[at + DOWN : at + DOWN + UP, :] = up[j * UP : j * UP + UP, :]
        out_ref[near] = slot[...].astype(BF)


def add_near(parts_ref, out_ref, total, slot):
    total[...] = sum_parts(parts_ref)
    slot[...] = jnp.zeros_like(slot)
    for zq in range(N_ZQ):
        at = zq * (DOWN + UP)
        slot[0:DOWN, :] = total[at : at + DOWN, :]
        slot[UP_AT : UP_AT + UP, :] = total[at + DOWN : at + DOWN + UP, :]
        out_ref[zq] = slot[...].astype(BF)


def update(
    parts_ref, dm_ref, df_ref, ds_ref, um_ref, uf_ref, us_ref,
    dm_out, df_out, ds_out, um_out, uf_out, us_out, down_send, up_send, slot,
):
    total = sum_parts(parts_ref)
    down_new = adamw_update(
        dm_ref[:, 0, :], df_ref[:, 0, :], ds_ref[:, 0, :], total[0:DOWN]
    )
    up_new = adamw_update(
        um_ref[:, 0, :], uf_ref[:, 0, :], us_ref[:, 0, :], total[UP_AT : UP_AT + UP]
    )
    dm_out[:, 0, :], df_out[:, 0, :], ds_out[:, 0, :] = down_new
    um_out[:, 0, :], uf_out[:, 0, :], us_out[:, 0, :] = up_new
    slot[...] = jnp.zeros_like(slot)
    slot[0:DOWN, :] = down_new[0]
    slot[UP_AT : UP_AT + UP, :] = up_new[0]
    down_send[...] = slot[0:UP_AT, :].astype(BF)
    value = slot[UP_AT:SLOT, :].astype(BF)
    for j in range(N_DP):
        up_send[j] = value


def merge(down_ref, up_ref, base_ref, out_ref, down, up):
    unpack(down_ref, down, DOWN)
    unpack(up_ref, up, UP)
    difference = lax.dot_general(
        up[...].astype(BF),
        down[...].astype(BF),
        (((1,), (1,)), ((), ())),
        preferred_element_type=F32,
    )
    out_ref[...] = (base_ref[...].astype(F32) + adapter_scale_factor * difference).astype(BF)


def spread_rows(rows_ref, out_ref):
    value = rows_ref[...]
    for j in range(out_ref.shape[0]):
        out_ref[j] = value


def owner_to_base(i):
    dp, mp = divmod(i, N_MP)
    y_lo, z = divmod(dp, N_Z)
    return (2 * mp + y_lo) * N_MP + z


def shards(
    activations,
    cotangent,
    resident_key_value_weight,
    down_master,
    down_first,
    down_second,
    up_master,
    up_first,
    up_second,
):
    tokens, features = activations.shape
    heads = cotangent.shape[1]
    shape = jax.ShapeDtypeStruct
    dp, mp = ("yl", "zq", "zp"), ("xy", "core")
    cotangent_t = cotangent.T
    base_t = resident_key_value_weight.T
    state = [a.reshape(DOWN, 1, RANK) for a in (down_master, down_first, down_second)]
    state += [a.reshape(UP, 1, RANK) for a in (up_master, up_first, up_second)]

    def exchange(value, axes):
        return lax.all_to_all(value, axes, 0, 0, tiled=True)

    def wide(rows):
        return pltpu.VMEM((rows, RANK), F32)

    activations, cotangent_t = kernel_call(
        fetch,
        [shape(activations.shape, BF), shape(cotangent_t.shape, BF)],
        2,
        limit=32 * 2**20,
    )(activations, cotangent_t)
    own = kernel_call(spread_factors, shape((N_Z, SLOT, RANK), BF), 2, [wide(SLOT)])(
        state[0], state[3]
    )
    factors = lax.all_gather(exchange(own, ("zq", "zp")), "yl", axis=0, tiled=True)
    core = lax.axis_index("core").astype(jnp.int32).reshape(1)
    half = shape((N_MP // N_CORE, tokens // N_MP, 2 * RANK), BF)
    other_half, a_use, bt_use = kernel_call(
        project_other,
        [half, shape((features, RANK), BF), shape((heads, RANK), BF)],
        4,
        [wide(features), wide(heads)],
        smem=(0,),
    )(core, factors, activations, cotangent_t)
    other_half = lax.ppermute(other_half, "core", [(0, 1), (1, 0)])
    own_half = kernel_call(project_own, half, 5, smem=(0,))(
        core, a_use, bt_use, activations, cotangent_t
    )
    own_half = kernel_call(add_pair, half, 2)(own_half, other_half)
    own_half = exchange(own_half, "xy")
    own_half = exchange(kernel_call(add_parts, half, 1)(own_half), "xy")
    full = lax.all_gather(own_half, "core", axis=0, tiled=True)
    near_rows = N_ZQ * (DOWN + UP)
    grads = kernel_call(
        gradients,
        shape((N_YL * N_ZP, near_rows, RANK), BF),
        3,
        [wide(features), wide(heads), wide(near_rows)],
    )(full, activations, cotangent_t)
    grads = exchange(grads, ("yl", "zp"))
    grads = kernel_call(
        add_near, shape((N_ZQ, SLOT, RANK), BF), 1, [wide(near_rows), wide(SLOT)]
    )(grads)
    grads = exchange(grads, "zq")
    *new, down_send, up_send = kernel_call(
        update,
        [shape(a.shape, F32) for a in state]
        + [shape((UP_AT, RANK), BF), shape((N_DP, SLOT - UP_AT, RANK), BF)],
        7,
        [wide(SLOT)],
    )(grads, *state)
    devices = N_DP * N_MP
    down_piece = lax.ppermute(
        down_send, dp + mp, [(i, owner_to_base(i)) for i in range(devices)]
    )
    up_rows = exchange(up_send, dp)
    down_piece, up_rows = lax.optimization_barrier((down_piece, up_rows))
    pieces = kernel_call(spread_rows, shape((N_MP, UP_AT, RANK), BF), 1)(down_piece)
    down_rows = exchange(pieces, mp)
    merged = kernel_call(
        merge, shape(base_t.shape, BF), 3, [wide(N_Z * DOWN), wide(heads)]
    )(down_rows, up_rows, base_t)
    return (merged.T, *[a.reshape(1, a.shape[0], RANK) for a in new])


def solution(mesh):
    sizes = (N_YL, N_ZQ, N_ZP, N_MP // N_CORE, N_CORE)
    fine = Mesh(mesh.devices.reshape(sizes), ("yl", "zq", "zp", "xy", "core"))
    dp, mp = ("yl", "zq", "zp"), ("xy", "core")
    wide, state = P(dp, mp), P(mp, dp, None)
    return jax.shard_map(
        shards,
        mesh=fine,
        in_specs=(wide,) * 3 + (state,) * 6,
        out_specs=(wide,) + (state,) * 6,
        check_vma=False,
    )
```

```python
import jax
import jax.numpy as jnp
from jax import lax
from jax.experimental import pallas as pl
from jax.experimental.pallas import tpu as pltpu
from jax.sharding import Mesh
from jax.sharding import PartitionSpec as P

adapter_scale_factor = 2.0
learn_rate = 0.05
beta_one = 0.9
beta_two = 0.999
adam_eps = 1e-08
decay_rate = 0.01
step_count = 10.0

BF = jnp.bfloat16
F32 = jnp.float32
DOWN, UP, UP_AT, SLOT = 36, 6, 40, 48
N_YL, N_Z, N_MP = 2, 16, 16
N_DP = N_YL * N_Z
N_CORE = 2
N_ZQ, N_ZP = 8, 2
RANK = 128

VMEM = pl.BlockSpec(memory_space=pltpu.VMEM)
HBM = pl.BlockSpec(memory_space=pltpu.HBM)
SMEM = pl.BlockSpec(memory_space=pltpu.SMEM)


def adamw_update(master, first, second, grad):
    first_new = beta_one * first + (1.0 - beta_one) * grad
    second_new = beta_two * second + (1.0 - beta_two) * grad * grad
    first_hat = first_new / (1.0 - beta_one**step_count)
    second_hat = second_new / (1.0 - beta_two**step_count)
    master_new = master - learn_rate * (
        first_hat / (jnp.sqrt(second_hat) + adam_eps) + decay_rate * master
    )
    return (master_new, first_new, second_new)


def kernel_call(body, out_shape, n_in, scratch=(), smem=(), hbm=(), limit=32 * 2**20):
    many = isinstance(out_shape, (list, tuple))
    return pl.pallas_call(
        body,
        out_shape=out_shape,
        in_specs=[SMEM if i in smem else HBM if i in hbm else VMEM for i in range(n_in)],
        out_specs=[VMEM] * len(out_shape) if many else VMEM,
        scratch_shapes=list(scratch),
        compiler_params=pltpu.CompilerParams(vmem_limit_bytes=limit),
    )


def spread_factors(down_ref, up_ref, out_ref, slot):
    slot[...] = jnp.zeros_like(slot)
    slot[0:DOWN, :] = down_ref[:, 0, :]
    slot[UP_AT : UP_AT + UP, :] = up_ref[:, 0, :]
    value = slot[...].astype(BF)
    for j in range(out_ref.shape[0]):
        out_ref[j] = value


def unpack(slots_ref, factor, rows, at=0):
    for j in range(slots_ref.shape[0]):
        factor[j * rows : j * rows + rows, :] = slots_ref[j].astype(F32)[at : at + rows]


def fetch(act_in, cot_in, act_ref, cot_ref):
    act_ref[...] = act_in[...]
    cot_ref[...] = cot_in[...]


def project_half(half, a_use, bt_use, act_ref, cot_ref, out_ref):
    groups, rows, _ = out_ref.shape
    tokens = groups * rows
    first = pl.multiple_of(half * tokens, tokens)
    back = lax.dot_general(
        cot_ref[:, pl.ds(first, tokens)],
        bt_use,
        (((0,), (0,)), ((), ())),
        preferred_element_type=F32,
    )
    out_ref[:, :, RANK:] = back.astype(BF).reshape(groups, rows, RANK)
    step = groups // 2
    for i in range(0, groups, step):
        at = pl.ds(pl.multiple_of(first + i * rows, step * rows), step * rows)
        hidden = jnp.dot(act_ref[at, :], a_use, preferred_element_type=F32)
        out_ref[i : i + step, :, 0:RANK] = hidden.astype(BF).reshape(step, rows, RANK)


def project_other(slots_ref, slots_other_ref, act_ref, cot_ref, out_ref, a_ref, bt_ref, down, up):
    low = lax.axis_index("yl") == 0
    for z in range(N_Z):
        own, other = slots_ref[z].astype(F32), slots_other_ref[z].astype(F32)
        for j, value in ((z, jnp.where(low, own, other)), (N_Z + z, jnp.where(low, other, own))):
            down[j * DOWN : j * DOWN + DOWN, :] = value[0:DOWN]
            up[j * UP : j * UP + UP, :] = value[UP_AT : UP_AT + UP]
    a_ref[...] = down[...].astype(BF)
    bt_ref[...] = up[...].astype(BF)
    project_half(1 - lax.axis_index("core"), a_ref[...], bt_ref[...], act_ref, cot_ref, out_ref)


def project_own(a_ref, bt_ref, act_ref, cot_ref, out_ref):
    project_half(lax.axis_index("core"), a_ref[...], bt_ref[...], act_ref, cot_ref, out_ref)


def sum_parts(parts_ref):
    total = parts_ref[0].astype(F32)
    for j in range(1, parts_ref.shape[0]):
        total += parts_ref[j].astype(F32)
    return total


def add_parts(parts_ref, out_ref):
    value = sum_parts(parts_ref).astype(BF)
    for j in range(out_ref.shape[0]):
        out_ref[j] = value


def add_pair(one_ref, two_ref, out_ref):
    out_ref[...] = (one_ref[...].astype(F32) + two_ref[...].astype(F32)).astype(BF)


def gradients(full_ref, act_ref, cot_ref, out_ref, down, up, slot):
    tokens = act_ref.shape[0]
    full = full_ref[...].reshape(tokens, 2 * RANK)
    hidden, back = full[:, 0:RANK], full[:, RANK:]
    down[...] = adapter_scale_factor * lax.dot_general(
        act_ref[...], back, (((0,), (0,)), ((), ())), preferred_element_type=F32
    )
    up[...] = adapter_scale_factor * jnp.dot(
        cot_ref[...], hidden, preferred_element_type=F32
    )
    for near in range(N_YL * N_ZP):
        y_lo, zp = divmod(near, N_ZP)
        for zq in range(N_ZQ):
            j = y_lo * N_Z + zq * N_ZP + zp
            at = zq * (DOWN + UP)
            slot[at : at + DOWN, :] = down[j * DOWN : j * DOWN + DOWN, :]
            slot[at + DOWN : at + DOWN + UP, :] = up[j * UP : j * UP + UP, :]
        out_ref[near] = slot[...].astype(BF)


def add_near(parts_ref, out_ref, total, slot):
    total[...] = sum_parts(parts_ref)
    slot[...] = jnp.zeros_like(slot)
    for zq in range(N_ZQ):
        at = zq * (DOWN + UP)
        slot[0:DOWN, :] = total[at : at + DOWN, :]
        slot[UP_AT : UP_AT + UP, :] = total[at + DOWN : at + DOWN + UP, :]
        out_ref[zq] = slot[...].astype(BF)


def update(
    parts_ref, dm_ref, df_ref, ds_ref, um_ref, uf_ref, us_ref,
    dm_out, df_out, ds_out, um_out, uf_out, us_out, down_send, up_send, slot,
):
    total = sum_parts(parts_ref)
    down_new = adamw_update(
        dm_ref[:, 0, :], df_ref[:, 0, :], ds_ref[:, 0, :], total[0:DOWN]
    )
    up_new = adamw_update(
        um_ref[:, 0, :], uf_ref[:, 0, :], us_ref[:, 0, :], total[UP_AT : UP_AT + UP]
    )
    dm_out[:, 0, :], df_out[:, 0, :], ds_out[:, 0, :] = down_new
    um_out[:, 0, :], uf_out[:, 0, :], us_out[:, 0, :] = up_new
    slot[...] = jnp.zeros_like(slot)
    slot[0:DOWN, :] = down_new[0]
    slot[UP_AT : UP_AT + UP, :] = up_new[0]
    down_send[...] = slot[0:UP_AT, :].astype(BF)
    value = slot[UP_AT:SLOT, :].astype(BF)
    for j in range(N_DP):
        up_send[j] = value


def merge(down_ref, up_ref, base_ref, out_ref, down, up):
    block = lax.axis_index("yl") * N_Z + lax.axis_index("zq") * N_ZP + lax.axis_index("zp")
    for z in range(N_Z):
        down[z * DOWN : z * DOWN + DOWN, :] = down_ref[base_slot(block, z)].astype(F32)[0:DOWN]
    unpack(up_ref, up, UP)
    difference = lax.dot_general(
        up[...].astype(BF),
        down[...].astype(BF),
        (((1,), (1,)), ((), ())),
        preferred_element_type=F32,
    )
    out_ref[...] = (base_ref[...].astype(F32) + adapter_scale_factor * difference).astype(BF)


def hold(value_ref, out_ref):
    out_ref[...] = value_ref[...]


def spread_rows(rows_ref, out_ref):
    value = rows_ref[...]
    for j in range(out_ref.shape[0]):
        out_ref[j] = value


NEAR_X = sum(v << 2 * i for i, v in enumerate((0, 1, 3, 0, 2, 1, 3, 2)))
NEAR_Y = sum(v << 2 * i for i, v in enumerate((0, 0, 0, 1, 0, 1, 1, 1)))


def base_slot(block, z):
    turn = (z - block % N_Z + 2 * N_Z - 1) % N_Z - (N_Z // 2 - 1)
    farther, nearer = -2 * turn, 2 * turn - 1
    rank = max(farther, nearer) if isinstance(turn, int) else jnp.maximum(farther, nearer)
    place = 2 * (rank // 2)
    owner = block // 2
    x = (owner // 4 + ((NEAR_X >> place) & 3)) % 4
    y = (owner // 2 + ((NEAR_Y >> place) & 3)) % 2
    return x * 4 + y * 2 + rank % 2


def owner_to_base(i):
    dp, mp = divmod(i, N_MP)
    y_lo, z = divmod(dp, N_Z)
    block = 2 * mp + y_lo
    return block * N_MP + base_slot(block, z)


def shards(
    activations,
    cotangent,
    resident_key_value_weight,
    down_master,
    down_first,
    down_second,
    up_master,
    up_first,
    up_second,
):
    tokens, features = activations.shape
    heads = cotangent.shape[1]
    shape = jax.ShapeDtypeStruct
    dp, mp = ("yl", "zq", "zp"), ("xy", "core")
    cotangent_t = cotangent.T
    base_t = resident_key_value_weight.T
    state = [a.reshape(DOWN, 1, RANK) for a in (down_master, down_first, down_second)]
    state += [a.reshape(UP, 1, RANK) for a in (up_master, up_first, up_second)]

    def exchange(value, axes):
        return lax.all_to_all(value, axes, 0, 0, tiled=True)

    def wide(rows):
        return pltpu.VMEM((rows, RANK), F32)

    activations, cotangent_t = kernel_call(
        fetch,
        [shape(activations.shape, BF), shape(cotangent_t.shape, BF)],
        2,
        limit=32 * 2**20,
    )(activations, cotangent_t)
    own = kernel_call(spread_factors, shape((N_Z, SLOT, RANK), BF), 2, [wide(SLOT)])(
        state[0], state[3]
    )
    factors = exchange(own, ("zq", "zp"))
    factors_other = lax.ppermute(factors, "yl", [(0, 1), (1, 0)])
    half = shape((N_MP // N_CORE, tokens // N_MP, 2 * RANK), BF)
    other_half, a_use, bt_use = kernel_call(
        project_other,
        [half, shape((features, RANK), BF), shape((heads, RANK), BF)],
        4,
        [wide(features), wide(heads)],
    )(factors, factors_other, activations, cotangent_t)
    other_half = lax.ppermute(other_half, "core", [(0, 1), (1, 0)])
    own_half = kernel_call(project_own, half, 4)(
        a_use, bt_use, activations, cotangent_t
    )
    own_half = kernel_call(add_pair, half, 2)(own_half, other_half)
    own_half = exchange(own_half, "xy")
    own_half = exchange(kernel_call(add_parts, half, 1)(own_half), "xy")
    full = lax.all_gather(own_half, "core", axis=0, tiled=True)
    near_rows = N_ZQ * (DOWN + UP)
    grads = kernel_call(
        gradients,
        shape((N_YL * N_ZP, near_rows, RANK), BF),
        3,
        [wide(features), wide(heads), wide(near_rows)],
    )(full, activations, cotangent_t)
    grads = exchange(grads, ("yl", "zp"))
    grads = kernel_call(
        add_near, shape((N_ZQ, SLOT, RANK), BF), 1, [wide(near_rows), wide(SLOT)]
    )(grads)
    grads = exchange(grads, "zq")
    *new, down_send, up_send = kernel_call(
        update,
        [shape(a.shape, F32) for a in state]
        + [shape((UP_AT, RANK), BF), shape((N_DP, SLOT - UP_AT, RANK), BF)],
        7,
        [wide(SLOT)],
    )(grads, *state)
    base_t, up_send = lax.optimization_barrier((base_t, up_send))
    base_t = kernel_call(hold, shape(base_t.shape, BF), 1)(base_t)
    devices = N_DP * N_MP
    down_piece = lax.ppermute(
        down_send, dp + mp, [(i, owner_to_base(i)) for i in range(devices)]
    )
    up_rows = exchange(up_send, dp)
    pieces = kernel_call(spread_rows, shape((N_MP, UP_AT, RANK), BF), 1)(down_piece)
    pieces, up_rows, base_t = lax.optimization_barrier((pieces, up_rows, base_t))
    down_rows = exchange(pieces, mp)
    merged = kernel_call(
        merge, shape(base_t.shape, BF), 3, [wide(N_Z * DOWN), wide(heads)]
    )(down_rows, up_rows, base_t)
    return (merged.T, *[a.reshape(1, a.shape[0], RANK) for a in new])


def solution(mesh):
    sizes = (N_YL, N_ZQ, N_ZP, N_MP // N_CORE, N_CORE)
    fine = Mesh(mesh.devices.reshape(sizes), ("yl", "zq", "zp", "xy", "core"))
    dp, mp = ("yl", "zq", "zp"), ("xy", "core")
    wide, state = P(dp, mp), P(mp, dp, None)
    return jax.shard_map(
        shards,
        mesh=fine,
        in_specs=(wide,) * 3 + (state,) * 6,
        out_specs=(wide,) + (state,) * 6,
        check_vma=False,
    )
```

```python
import jax
import jax.numpy as jnp
from jax import lax
from jax.experimental import pallas as pl
from jax.experimental.pallas import tpu as pltpu
from jax.sharding import Mesh
from jax.sharding import PartitionSpec as P

adapter_scale_factor = 2.0
learn_rate = 0.05
beta_one = 0.9
beta_two = 0.999
adam_eps = 1e-08
decay_rate = 0.01
step_count = 10.0

BF = jnp.bfloat16
F32 = jnp.float32
DOWN, UP, UP_AT, SLOT = 36, 6, 40, 48
N_YL, N_Z, N_MP = 2, 16, 16
N_DP = N_YL * N_Z
N_CORE = 2
N_ZQ, N_ZP = 8, 2
RANK = 128

VMEM = pl.BlockSpec(memory_space=pltpu.VMEM)
HBM = pl.BlockSpec(memory_space=pltpu.HBM)
SMEM = pl.BlockSpec(memory_space=pltpu.SMEM)


def adamw_update(master, first, second, grad):
    first_new = beta_one * first + (1.0 - beta_one) * grad
    second_new = beta_two * second + (1.0 - beta_two) * grad * grad
    first_hat = first_new / (1.0 - beta_one**step_count)
    second_hat = second_new / (1.0 - beta_two**step_count)
    master_new = master - learn_rate * (
        first_hat / (jnp.sqrt(second_hat) + adam_eps) + decay_rate * master
    )
    return (master_new, first_new, second_new)


def kernel_call(body, out_shape, n_in, scratch=(), smem=(), hbm=(), limit=12 * 2**20):
    many = isinstance(out_shape, (list, tuple))
    return pl.pallas_call(
        body,
        out_shape=out_shape,
        in_specs=[SMEM if i in smem else HBM if i in hbm else VMEM for i in range(n_in)],
        out_specs=[VMEM] * len(out_shape) if many else VMEM,
        scratch_shapes=list(scratch),
        compiler_params=pltpu.CompilerParams(vmem_limit_bytes=limit),
    )


def spread_factors(down_ref, up_ref, out_ref, slot):
    slot[...] = jnp.zeros_like(slot)
    slot[0:DOWN, :] = down_ref[:, 0, :]
    slot[UP_AT : UP_AT + UP, :] = up_ref[:, 0, :]
    value = slot[...].astype(BF)
    for j in range(out_ref.shape[0]):
        out_ref[j] = value


def unpack(slots_ref, factor, rows, at=0):
    for j in range(slots_ref.shape[0]):
        factor[j * rows : j * rows + rows, :] = slots_ref[j].astype(F32)[at : at + rows]


def fetch(act_in, cot_in, act_ref, cot_ref):
    act_ref[...] = act_in[...]
    cot_ref[...] = cot_in[...]


def project_half(half, a_use, bt_use, act_ref, cot_ref, out_ref):
    groups, rows, _ = out_ref.shape
    tokens = groups * rows
    first = pl.multiple_of(half * tokens, tokens)
    back = lax.dot_general(
        cot_ref[:, pl.ds(first, tokens)],
        bt_use,
        (((0,), (0,)), ((), ())),
        preferred_element_type=F32,
    )
    out_ref[:, :, RANK:] = back.astype(BF).reshape(groups, rows, RANK)
    step = groups // 2
    for i in range(0, groups, step):
        at = pl.ds(pl.multiple_of(first + i * rows, step * rows), step * rows)
        hidden = jnp.dot(act_ref[at, :], a_use, preferred_element_type=F32)
        out_ref[i : i + step, :, 0:RANK] = hidden.astype(BF).reshape(step, rows, RANK)


def project_other(slots_ref, slots_other_ref, act_ref, cot_ref, out_ref, a_ref, bt_ref, down, up):
    low = lax.axis_index("yl") == 0
    for z in range(N_Z):
        own, other = slots_ref[z].astype(F32), slots_other_ref[z].astype(F32)
        for j, value in ((z, jnp.where(low, own, other)), (N_Z + z, jnp.where(low, other, own))):
            down[j * DOWN : j * DOWN + DOWN, :] = value[0:DOWN]
            up[j * UP : j * UP + UP, :] = value[UP_AT : UP_AT + UP]
    a_ref[...] = down[...].astype(BF)
    bt_ref[...] = up[...].astype(BF)
    project_half(1 - lax.axis_index("core"), a_ref[...], bt_ref[...], act_ref, cot_ref, out_ref)


def project_own(a_ref, bt_ref, act_ref, cot_ref, out_ref):
    project_half(lax.axis_index("core"), a_ref[...], bt_ref[...], act_ref, cot_ref, out_ref)


def sum_parts(parts_ref):
    total = parts_ref[0].astype(F32)
    for j in range(1, parts_ref.shape[0]):
        total += parts_ref[j].astype(F32)
    return total


def add_parts(parts_ref, out_ref):
    value = sum_parts(parts_ref).astype(BF)
    for j in range(out_ref.shape[0]):
        out_ref[j] = value


def add_pair(one_ref, two_ref, out_ref):
    out_ref[...] = (one_ref[...].astype(F32) + two_ref[...].astype(F32)).astype(BF)


def gradients(full_ref, act_ref, cot_ref, out_ref, down, up, slot):
    tokens = act_ref.shape[0]
    full = full_ref[...].reshape(tokens, 2 * RANK)
    hidden, back = full[:, 0:RANK], full[:, RANK:]
    down[...] = adapter_scale_factor * lax.dot_general(
        act_ref[...], back, (((0,), (0,)), ((), ())), preferred_element_type=F32
    )
    up[...] = adapter_scale_factor * jnp.dot(
        cot_ref[...], hidden, preferred_element_type=F32
    )
    for near in range(N_YL * N_ZP):
        y_lo, zp = divmod(near, N_ZP)
        for zq in range(N_ZQ):
            j = y_lo * N_Z + zq * N_ZP + zp
            at = zq * (DOWN + UP)
            slot[at : at + DOWN, :] = down[j * DOWN : j * DOWN + DOWN, :]
            slot[at + DOWN : at + DOWN + UP, :] = up[j * UP : j * UP + UP, :]
        out_ref[near] = slot[...].astype(BF)


def add_near(parts_ref, out_ref, total, slot):
    total[...] = sum_parts(parts_ref)
    slot[...] = jnp.zeros_like(slot)
    for zq in range(N_ZQ):
        at = zq * (DOWN + UP)
        slot[0:DOWN, :] = total[at : at + DOWN, :]
        slot[UP_AT : UP_AT + UP, :] = total[at + DOWN : at + DOWN + UP, :]
        out_ref[zq] = slot[...].astype(BF)


def update(
    parts_ref, dm_ref, df_ref, ds_ref, um_ref, uf_ref, us_ref,
    dm_out, df_out, ds_out, um_out, uf_out, us_out, down_send, up_send, slot,
):
    total = sum_parts(parts_ref)
    down_new = adamw_update(
        dm_ref[:, 0, :], df_ref[:, 0, :], ds_ref[:, 0, :], total[0:DOWN]
    )
    up_new = adamw_update(
        um_ref[:, 0, :], uf_ref[:, 0, :], us_ref[:, 0, :], total[UP_AT : UP_AT + UP]
    )
    dm_out[:, 0, :], df_out[:, 0, :], ds_out[:, 0, :] = down_new
    um_out[:, 0, :], uf_out[:, 0, :], us_out[:, 0, :] = up_new
    slot[...] = jnp.zeros_like(slot)
    slot[0:DOWN, :] = down_new[0]
    slot[UP_AT : UP_AT + UP, :] = up_new[0]
    down_send[...] = slot[0:UP_AT, :].astype(BF)
    value = slot[UP_AT:SLOT, :].astype(BF)
    for j in range(N_DP):
        up_send[j] = value


def merge(down_ref, up_ref, base_ref, out_ref, down, up):
    block = lax.axis_index("yl") * N_Z + lax.axis_index("zq") * N_ZP + lax.axis_index("zp")
    for z in range(N_Z):
        down[z * DOWN : z * DOWN + DOWN, :] = down_ref[base_slot(block, z)].astype(F32)[0:DOWN]
    unpack(up_ref, up, UP)
    difference = lax.dot_general(
        up[...].astype(BF),
        down[...].astype(BF),
        (((1,), (1,)), ((), ())),
        preferred_element_type=F32,
    )
    out_ref[...] = (base_ref[...].astype(F32) + adapter_scale_factor * difference).astype(BF)


def hold(value_ref, out_ref):
    out_ref[...] = value_ref[...]


def spread_rows(rows_ref, out_ref):
    value = rows_ref[...]
    for j in range(out_ref.shape[0]):
        out_ref[j] = value


NEAR_X = sum(v << 2 * i for i, v in enumerate((0, 1, 3, 0, 2, 1, 3, 2)))
NEAR_Y = sum(v << 2 * i for i, v in enumerate((0, 0, 0, 1, 0, 1, 1, 1)))


def base_slot(block, z):
    turn = (z - block % N_Z + 2 * N_Z - 1) % N_Z - (N_Z // 2 - 1)
    farther, nearer = -2 * turn, 2 * turn - 1
    rank = max(farther, nearer) if isinstance(turn, int) else jnp.maximum(farther, nearer)
    place = 2 * (rank // 2)
    owner = block // 2
    x = (owner // 4 + ((NEAR_X >> place) & 3)) % 4
    y = (owner // 2 + ((NEAR_Y >> place) & 3)) % 2
    return x * 4 + y * 2 + rank % 2


def owner_to_base(i):
    dp, mp = divmod(i, N_MP)
    y_lo, z = divmod(dp, N_Z)
    block = 2 * mp + y_lo
    return block * N_MP + base_slot(block, z)


def shards(
    activations,
    cotangent,
    resident_key_value_weight,
    down_master,
    down_first,
    down_second,
    up_master,
    up_first,
    up_second,
):
    tokens, features = activations.shape
    heads = cotangent.shape[1]
    shape = jax.ShapeDtypeStruct
    dp, mp = ("yl", "zq", "zp"), ("xy", "core")
    cotangent_t = cotangent.T
    base_t = resident_key_value_weight.T
    state = [a.reshape(DOWN, 1, RANK) for a in (down_master, down_first, down_second)]
    state += [a.reshape(UP, 1, RANK) for a in (up_master, up_first, up_second)]

    def exchange(value, axes):
        return lax.all_to_all(value, axes, 0, 0, tiled=True)

    def wide(rows):
        return pltpu.VMEM((rows, RANK), F32)

    activations, cotangent_t = kernel_call(
        fetch,
        [shape(activations.shape, BF), shape(cotangent_t.shape, BF)],
        2,
        limit=12 * 2**20,
    )(activations, cotangent_t)
    own = kernel_call(spread_factors, shape((N_Z, SLOT, RANK), BF), 2, [wide(SLOT)])(
        state[0], state[3]
    )
    factors = exchange(own, ("zq", "zp"))
    factors_other = lax.ppermute(factors, "yl", [(0, 1), (1, 0)])
    half = shape((N_MP // N_CORE, tokens // N_MP, 2 * RANK), BF)
    other_half, a_use, bt_use = kernel_call(
        project_other,
        [half, shape((features, RANK), BF), shape((heads, RANK), BF)],
        4,
        [wide(features), wide(heads)],
    )(factors, factors_other, activations, cotangent_t)
    other_half = lax.ppermute(other_half, "core", [(0, 1), (1, 0)])
    own_half = kernel_call(project_own, half, 4)(
        a_use, bt_use, activations, cotangent_t
    )
    own_half = kernel_call(add_pair, half, 2)(own_half, other_half)
    own_half = exchange(own_half, "xy")
    own_half = exchange(kernel_call(add_parts, half, 1)(own_half), "xy")
    full = lax.all_gather(own_half, "core", axis=0, tiled=True)
    near_rows = N_ZQ * (DOWN + UP)
    grads = kernel_call(
        gradients,
        shape((N_YL * N_ZP, near_rows, RANK), BF),
        3,
        [wide(features), wide(heads), wide(near_rows)],
    )(full, activations, cotangent_t)
    grads = exchange(grads, ("yl", "zp"))
    grads = kernel_call(
        add_near, shape((N_ZQ, SLOT, RANK), BF), 1, [wide(near_rows), wide(SLOT)]
    )(grads)
    grads = exchange(grads, "zq")
    *new, down_send, up_send = kernel_call(
        update,
        [shape(a.shape, F32) for a in state]
        + [shape((UP_AT, RANK), BF), shape((N_DP, SLOT - UP_AT, RANK), BF)],
        7,
        [wide(SLOT)],
    )(grads, *state)
    base_t, up_send = lax.optimization_barrier((base_t, up_send))
    base_t = kernel_call(hold, shape(base_t.shape, BF), 1)(base_t)
    devices = N_DP * N_MP
    down_piece = lax.ppermute(
        down_send, dp + mp, [(i, owner_to_base(i)) for i in range(devices)]
    )
    up_rows = exchange(up_send, dp)
    pieces = kernel_call(spread_rows, shape((N_MP, UP_AT, RANK), BF), 1)(down_piece)
    pieces, up_rows, base_t = lax.optimization_barrier((pieces, up_rows, base_t))
    down_rows = exchange(pieces, mp)
    merged = kernel_call(
        merge, shape(base_t.shape, BF), 3, [wide(N_Z * DOWN), wide(heads)]
    )(down_rows, up_rows, base_t)
    return (merged.T, *[a.reshape(1, a.shape[0], RANK) for a in new])


def solution(mesh):
    sizes = (N_YL, N_ZQ, N_ZP, N_MP // N_CORE, N_CORE)
    fine = Mesh(mesh.devices.reshape(sizes), ("yl", "zq", "zp", "xy", "core"))
    dp, mp = ("yl", "zq", "zp"), ("xy", "core")
    wide, state = P(dp, mp), P(mp, dp, None)
    return jax.shard_map(
        shards,
        mesh=fine,
        in_specs=(wide,) * 3 + (state,) * 6,
        out_specs=(wide,) + (state,) * 6,
        check_vma=False,
    )
```
